512 devices in a mesh: dp: 16 (over y, x), expert: 32 (over z, core).
Axes of the slice: x: 4, y: 4, z: 16, core: 2. Of those that a mesh axis runs over, the one named last changes fastest.
Arguments:
- tokens: bfloat16 [16384, 2048], P(('dp', 'expert')), may hold values from -6 to 6
- routes: int32 [16384, 8], P(('dp', 'expert')), may hold values from 0 to 31, all different within a row; in each aligned block of 32 rows (0 to 31, 32 to 63, ...) at most 12 rows name the same one
- gates: float32 [16384, 8], P(('dp', 'expert')), may hold values from 0.05 to 0.5
- curvature: float32 [16384], P(('dp', 'expert')), may hold values from 0.25 to 4
- w_gate: bfloat16 [32, 2048, 768], P('expert', 'dp'), may hold values from -0.125 to 0.125
- w_up: bfloat16 [32, 2048, 768], P('expert', 'dp'), may hold values from -0.125 to 0.125
- direction: bfloat16 [32, 2048, 768], P('expert', 'dp'), may hold values from -0.21875 to 0.21875
Outputs:
- output_tangent: bfloat16 [16384, 2048], P(('dp', 'expert'))
- curvature_product: bfloat16 [32, 2048, 768], P('expert', 'dp')
The draws below stay inside these ranges and needn't reach their ends.
Inputs may be any that keep to these rules, and one draw needn't show every extreme that they name: `routes`: the 8 ids of a token differ. Among the tokens of one device no expert is named by more than 12 tokens, a bound that some block reaches of them.
All inputs are finite; a program needn't handle non-finite values.
Results may differ from the reference program's by a relative error of at most 0.017.
Values may be sent and summed in bfloat16 or wider, within the bound.
No kernel may reach another device: no remote copies, remote signals or barrier semaphores. Data moves between devices by JAX's collectives and lax.ppermute only.
A program may use at most 64 MiB of HBM per device.

```python
import math
import jax
import jax.numpy as jnp
import numpy as np
from jax import lax

D = 2048
F = 768
TOP = 8
TOK_DEV = 32
EXPERTS = 32
CAP = 12
TOKENS = 16384
N_DP = 16
N_EXPERT = 32


def block_levels(stream_key, shape, shards, smallest, high):
    gain = 1.0
    for position, shards_of in shards:
        steps = jax.random.uniform(jax.random.fold_in(jax.random.fold_in(stream_key, 6), position), (shards_of,), jnp.float32, smallest / len(shards), high / len(shards))
        gain = gain * jnp.repeat(jnp.exp(steps), shape[position] // shards_of).reshape((-1,) + (1,) * (len(shape) - 1 - position))
    return gain


def routed_block(rng, own, number, rows, count, top, reach, slope):
    order = jax.random.permutation(rng, count)
    heavy_load, ordinary = portions_of(count, rows * top, reach, slope, True), portions_of(count, rows * top, reach, slope, False)
    places = jnp.arange(count)

    def named(tallies, turn):
        used = int((tallies > 0).sum())
        fixed = max(1, used // 4)
        shifted = fixed + (places - fixed + turn * (used - fixed)) % max(1, count - fixed)
        return jnp.zeros((count,), jnp.int32).at[order[jnp.where(places < fixed, places, shifted)]].set(jnp.asarray(tallies, jnp.int32))

    tallies = jnp.where(number % 4 == 0, named(heavy_load, number // 4), named(ordinary, number - number // 4 - 1))
    mixed = jax.random.permutation(jax.random.fold_in(own, 3), count)
    donor, taker = mixed[0:count // 2 * 2:2], mixed[1:count // 2 * 2:2]
    margin = jnp.minimum(tallies[donor] - 1, reach - tallies[taker]) // 2
    margin = jnp.where((donor == order[0]) | (taker == order[0]) | (tallies[taker] == 0), 0, jnp.maximum(margin, 0))
    shifted = jax.random.randint(jax.random.fold_in(own, 4), (count // 2,), 0, 1 << 20) % (margin + 1)
    tallies = tallies.at[donor].add(-shifted).at[taker].add(shifted)
    items = jnp.searchsorted(jnp.cumsum(tallies), jnp.arange(rows * top), side="right").astype(jnp.int32)
    table = items.reshape(top, rows).T
    table = table[jax.random.permutation(jax.random.fold_in(own, 1), rows)]
    turn = jax.random.randint(jax.random.fold_in(own, 2), (rows, 1), 0, top)
    return jnp.take_along_axis(table, (jnp.arange(top)[None, :] + turn) % top, axis=1)


def portions_of(count, total, most, skew, full):
    weights = [(1 << 20) // math.isqrt(standing ** skew) + 1 for standing in range(1, count + 1)]
    largest = most if full else min(most, max(-(-total // count), total * weights[0] // sum(weights)))
    least = 1 if total - largest >= count - 1 else 0
    counts, rest = [largest] + [least] * (count - 1), total - largest - least * (count - 1)
    while rest > 0:
        movable = [i for i in range(1, count) if counts[i] < largest] or [i for i in range(1, count) if counts[i] < most]
        pool, remaining = sum([weights[i] for i in movable]), rest
        for i in movable:
            addition = min(most - counts[i], max(1, remaining * weights[i] // pool), rest)
            counts[i] = counts[i] + addition
            rest = rest - addition
    return np.array(counts)


def scatter_about(stream_key, shape, scale, most, cuts=(), kind=jnp.bfloat16):
    factor_of = block_levels(stream_key, shape, cuts, -0.22, 0.18) if cuts else 1.0
    array = jax.random.normal(stream_key, shape, jnp.float32) * scale * factor_of
    return jnp.minimum(jnp.maximum(array, -most), most).astype(kind)


def setup_inputs(seed: int = 0) -> dict:
    seeds = jax.random.split(jax.random.key(seed), 8)
    tokens = scatter_about(seeds[0], (TOKENS, D), 1.0, 6.0, ((0, 512),))
    routes_keys = jax.random.split(jax.random.fold_in(seeds[1], 1), TOKENS // TOK_DEV)
    routes_turns = jax.random.permutation(jax.random.fold_in(seeds[1], 3), TOKENS // TOK_DEV)
    routes = jax.vmap(lambda own, number: routed_block(jax.random.fold_in(seeds[1], 2), own, number, TOK_DEV, EXPERTS, TOP, CAP, 2))(routes_keys, routes_turns).reshape((TOKENS, TOP))
    gates = jnp.clip(jnp.exp(math.log(0.5) - 2.3025851 * jax.random.uniform(seeds[2], (TOKENS, TOP), jnp.float32) ** block_levels(seeds[2], (TOKENS, TOP), ((0, 512),), -0.2, 0.2)), 0.05, 0.5)
    curvature = jnp.clip(jnp.exp(math.log(4.0) - 2.7725887 * jax.random.uniform(seeds[3], (TOKENS,), jnp.float32) ** block_levels(seeds[3], (TOKENS,), ((0, 512),), -0.2, 0.2)), 0.25, 4.0)
    w_gate = scatter_about(seeds[4], (EXPERTS, D, F), D ** -0.5, 0.125, ((0, 32), (1, 16)))
    w_up = scatter_about(seeds[5], (EXPERTS, D, F), D ** -0.5, 0.125, ((0, 32), (1, 16)))
    direction = scatter_about(seeds[6], (EXPERTS, D, F), F ** -0.5, 0.21875, ((0, 32), (1, 16)))
    return {"tokens": tokens, "routes": routes, "gates": gates, "curvature": curvature, "w_gate": w_gate, "w_up": w_up, "direction": direction}


def slots_of(route_block):
    flat = route_block.reshape(-1)
    onehot = (flat[:, None] == jnp.arange(EXPERTS, dtype=jnp.int32)[None, :]).astype(jnp.int32)
    before = jnp.cumsum(onehot, axis=0) - onehot
    return jnp.sum(before * onehot, axis=1).astype(jnp.int32)


def reference(tokens, routes, gates, curvature, w_gate, w_up, direction):
    sources = N_EXPERT
    group_tokens = tokens.reshape(N_DP, sources * TOK_DEV, D)
    group_routes = routes.reshape(N_DP, sources, TOK_DEV, TOP)
    group_gates = gates.reshape(N_DP, sources * TOK_DEV, TOP)
    group_curv = curvature.reshape(N_DP, sources * TOK_DEV)

    def one_group(total, inputs):
        x_rows, route_blocks, gate_rows, curv_rows = inputs
        slots = jax.vmap(slots_of)(route_blocks).reshape(-1)
        chosen = route_blocks.reshape(-1).astype(jnp.int32)
        source = jnp.repeat(jnp.arange(sources, dtype=jnp.int32), TOK_DEV * TOP)
        x_rep = jnp.repeat(x_rows, TOP, axis=0)
        buffer = jnp.zeros((EXPERTS, sources, CAP, D), jnp.bfloat16).at[chosen, source, slots].set(x_rep)

        def per_expert(args):
            rows, wg, wu, vd = args
            rows = rows.reshape(sources * CAP, D)
            gate_pre = jnp.dot(rows, wg, preferred_element_type=jnp.float32)
            up_pre = jnp.dot(rows, wu, preferred_element_type=jnp.float32)
            hidden = (jax.nn.silu(gate_pre) * up_pre).astype(jnp.bfloat16)
            tangent = jnp.dot(hidden, vd.T, preferred_element_type=jnp.float32).astype(jnp.bfloat16)
            return hidden, tangent

        hidden, tangent = lax.map(per_expert, (buffer, w_gate, w_up, direction))
        picked = tangent.reshape(EXPERTS, sources, CAP, D)[chosen, source, slots]
        picked = picked.reshape(sources * TOK_DEV, TOP, D).astype(jnp.float32)
        jv = jnp.sum(gate_rows[:, :, None] * picked, axis=1)
        scale = gate_rows * curv_rows[:, None]
        weighted = (scale[:, :, None] * jv[:, None, :]).astype(jnp.bfloat16).reshape(-1, D)
        wbuffer = jnp.zeros((EXPERTS, sources, CAP, D), jnp.bfloat16).at[chosen, source, slots].set(weighted)

        def per_part(args):
            wrows, hrows = args
            wrows = wrows.reshape(sources * CAP, D).astype(jnp.float32)
            return jnp.dot(wrows.T, hrows.astype(jnp.float32)).astype(jnp.bfloat16)

        parts = lax.map(per_part, (wbuffer, hidden))
        return total + parts.astype(jnp.float32), jv.astype(jnp.bfloat16)

    total, out_tangent = lax.scan(one_group, jnp.zeros((EXPERTS, D, F), jnp.float32),
                                  (group_tokens, group_routes, group_gates, group_curv))
    return out_tangent.reshape(TOKENS, D), total.astype(jnp.bfloat16)
```

```python
import jax
import jax.numpy as jnp
from jax import lax
from jax.sharding import Mesh, PartitionSpec as P

BF = jnp.bfloat16
F32 = jnp.float32


def fetch(value, axis, shift, size):
    return lax.ppermute(value, axis, [((i + shift) % size, i) for i in range(size)])


def ring4(value, axis):
    half = value.shape[-2] // 2
    after = fetch(value, axis, 1, 4)
    before = fetch(value, axis, -1, 4)
    low = fetch(after[..., :half, :], axis, 1, 4)
    high = fetch(before[..., half:, :], axis, -1, 4)
    return jnp.stack([value, after, jnp.concatenate([low, high], -2), before])


def turn(value, axis, start):
    doubled = jnp.concatenate([value, value], axis)
    return lax.dynamic_slice_in_dim(doubled, start, value.shape[axis], axis)


def to_relative(value, y, x):
    rows, width = value.shape
    value = turn(turn(value.reshape(rows, 4, 4, width // 16), 1, y), 2, x)
    first, second = jnp.split(value, 2, axis=3)
    second = second.swapaxes(1, 2)
    return jnp.concatenate([first.reshape(rows, -1), second.reshape(rows, -1)], 1)


def to_absolute(value, y, x):
    rows, width = value.shape
    first, second = jnp.split(value, 2, axis=1)
    first = first.reshape(rows, 4, 4, width // 32)
    second = second.reshape(rows, 4, 4, width // 32).swapaxes(1, 2)
    both = jnp.concatenate([first, second], 3)
    return turn(turn(both, 1, (4 - y) % 4), 2, (4 - x) % 4).reshape(rows, width)


def local(tokens, routes, gates, curvature, w_gate, w_up, direction):
    rows, width = tokens.shape
    hidden_width = w_gate.shape[2]
    z_count, cores = lax.axis_size("z"), lax.axis_size("c")
    experts = z_count * cores
    y, x, core = lax.axis_index("y"), lax.axis_index("x"), lax.axis_index("c")
    me = lax.axis_index(("z", "c"))

    chosen = routes[:, :, None] == jnp.arange(experts, dtype=jnp.int32)
    table = jnp.sum(jnp.where(chosen, gates[:, :, None], 0.0), axis=1)
    table_high = table.astype(BF)
    table_low = (table - table_high.astype(F32)).astype(BF)
    sent = jnp.concatenate(
        [
            to_relative(tokens, y, x),
            table_high,
            table_low,
            jnp.zeros((rows, 128 - 2 * experts), BF),
        ],
        1,
    )
    arrived = lax.all_gather(sent, ("z", "c"), axis=0, tiled=True)

    stacked = jnp.concatenate([w_gate[0], w_up[0], direction[0]], 1)
    half = stacked.shape[0] // 2
    first = ring4(ring4(stacked[:half], "x"), "y")
    second = ring4(ring4(stacked[half:], "y"), "x")
    weights = jnp.concatenate(
        [first.reshape(width // 2, -1), second.reshape(width // 2, -1)], 0
    )

    lanes = lax.broadcasted_iota(jnp.int32, (1, 128), 1)
    mine = (lanes == me) | (lanes == me + experts)
    share = jnp.sum(
        jnp.where(mine, arrived[:, width:].astype(F32), 0.0), axis=1, keepdims=True
    )
    group = arrived[:, :width]
    gate_pre = jnp.dot(group, weights[:, :hidden_width], preferred_element_type=F32)
    up_pre = jnp.dot(
        group, weights[:, hidden_width : 2 * hidden_width], preferred_element_type=F32
    )
    hidden = (jax.nn.silu(gate_pre) * up_pre * share).astype(BF)

    by_core = hidden.reshape(z_count, cores, rows, hidden_width)
    away = lax.dynamic_index_in_dim(by_core, 1 - core, 1, False).reshape(-1, hidden_width)
    home = lax.dynamic_index_in_dim(by_core, core, 1, False).reshape(-1, hidden_width)

    def tangent(part):
        return lax.dot_general(
            part,
            weights[:, 2 * hidden_width :],
            (((1,), (1,)), ((), ())),
            preferred_element_type=F32,
        )

    other = lax.ppermute(tangent(away).astype(BF), "c", [(0, 1), (1, 0)])
    paired = (tangent(home) + other.astype(F32)).astype(BF)
    jv = lax.psum_scatter(paired, "z", scatter_dimension=0, tiled=True)
    output_tangent = to_absolute(jv, y, x)
    curved = (curvature[:, None] * output_tangent.astype(F32)).astype(BF)
    spread = lax.all_gather(curved, ("z", "c"), axis=0, tiled=True)
    part = lax.dot_general(
        spread, hidden, (((0,), (0,)), ((), ())), preferred_element_type=F32
    ).astype(BF)

    def add_over(value, axis):
        value = value.reshape(4, -1, hidden_width)
        moved = lax.all_to_all(value, axis, 0, 0, tiled=True)
        return jnp.sum(moved.astype(F32), axis=0).astype(BF)

    product = add_over(add_over(part, "y"), "x")
    return output_tangent, product[None]


def solution(mesh):
    torus = Mesh(mesh.devices.reshape(4, 4, 16, 2), ("y", "x", "z", "c"))
    tokens = P(("y", "x", "z", "c"), None)
    matrix = P(("z", "c"), ("y", "x"), None)
    return jax.shard_map(
        local,
        mesh=torus,
        in_specs=(tokens, tokens, tokens, P(("y", "x", "z", "c")), matrix, matrix, matrix),
        out_specs=(tokens, matrix),
        check_vma=False,
    )
```

```python
import jax
import jax.numpy as jnp
from jax import lax
from jax.sharding import Mesh, PartitionSpec as P

BF = jnp.bfloat16
F32 = jnp.float32
FAR = (-6, -3, 0, 3, 6)


def fetch(value, axis, shift, size):
    return lax.ppermute(value, axis, [((i + shift) % size, i) for i in range(size)])


def swap_cores(value):
    return lax.ppermute(value, "c", [(0, 1), (1, 0)])


def ring4_one(value, axis):
    return value, fetch(value, axis, 1, 4), fetch(value, axis, -1, 4)


def ring4_two(hop, axis):
    value, ahead, behind = hop
    half = value.shape[-2] // 2
    low = fetch(ahead[..., :half, :], axis, 1, 4)
    high = fetch(behind[..., half:, :], axis, -1, 4)
    return jnp.stack([value, ahead, jnp.concatenate([low, high], -2), behind])


def ring4(value, axis):
    return ring4_two(ring4_one(value, axis), axis)


def turn(value, axis, start):
    doubled = jnp.concatenate([value, value], axis)
    return lax.dynamic_slice_in_dim(doubled, start, value.shape[axis], axis)


def to_relative(value, y, x):
    rows, width = value.shape
    value = turn(turn(value.reshape(rows, 4, 4, width // 16), 1, y), 2, x)
    first, second = jnp.split(value, 2, axis=3)
    second = second.swapaxes(1, 2)
    return jnp.concatenate([first.reshape(rows, -1), second.reshape(rows, -1)], 1)


def to_absolute(value, y, x, flip):
    rows, width = value.shape
    value = value.reshape(rows, 4, 4, width // 16)
    if flip:
        value = value.swapaxes(1, 2)
    return turn(turn(value, 1, (4 - y) % 4), 2, (4 - x) % 4)


def after(value, *others):
    return lax.optimization_barrier((value,) + others)[0]


def reduce_near(parts, rows):
    block, half = len(FAR) * rows, rows // 2
    behind, own, ahead, across = jnp.split(parts, [block, 2 * block, 3 * block])
    return (
        own,
        fetch(ahead, "z", -1, 16),
        fetch(behind, "z", 1, 16),
        fetch(across[:half], "z", -2, 16),
        fetch(across[half:], "z", 2, 16),
    )


def reduce_far(own, ahead, behind, low, high):
    half = low.shape[0]
    total = own.astype(F32) + ahead.astype(F32) + behind.astype(F32)
    pieces = jnp.split(total, len(FAR))
    pieces[0] = jnp.concatenate([pieces[0][:half], pieces[0][half:] + high.astype(F32)])
    pieces[-1] = jnp.concatenate([pieces[-1][:half] + low.astype(F32), pieces[-1][half:]])
    moved = [fetch(p.astype(BF), "z", -o, 16) if o else p for o, p in zip(FAR, pieces)]
    return moved


def spread_near(own, rows):
    half = rows // 2
    return (
        fetch(own, "z", -1, 16),
        own,
        fetch(own, "z", 1, 16),
        fetch(own[-rows:][:half], "z", 2, 16),
        fetch(own[:rows][half:], "z", -2, 16),
    )


def local(tokens, routes, gates, curvature, w_gate, w_up, direction):
    rows, width = tokens.shape
    hidden_width = w_gate.shape[2]
    z_count, cores = lax.axis_size("z"), lax.axis_size("c")
    experts = z_count * cores
    y, x, z, core = (lax.axis_index(name) for name in ("y", "x", "z", "c"))
    me = z * cores + core

    chosen = routes[:, :, None] == jnp.arange(experts, dtype=jnp.int32)
    table = jnp.sum(jnp.where(chosen, gates[:, :, None], 0.0), axis=1)
    table_high = table.astype(BF)
    table_low = (table - table_high.astype(F32)).astype(BF)
    sent = jnp.concatenate(
        [
            to_relative(tokens, y, x),
            table_high,
            table_low,
            jnp.zeros((rows, 128 - 2 * experts), BF),
        ],
        1,
    )
    arrived = lax.all_gather(sent, ("z", "c"), axis=0, tiled=True)

    stacked = jnp.concatenate([w_gate[0], w_up[0], direction[0]], 1)
    half = stacked.shape[0] // 2
    first = ring4(stacked[:half], "x")
    second = ring4(stacked[half:], "y")
    cut = 2 * hidden_width
    first_hop = ring4_one(first[..., :cut], "y")
    second_hop = ring4_one(second[..., :cut], "x")
    first_hop, second_hop, first_back, second_back = lax.optimization_barrier(
        (first_hop, second_hop, first[..., cut:], second[..., cut:])
    )
    first_in = ring4_two(first_hop, "y").reshape(width // 2, -1)
    second_in = ring4_two(second_hop, "x").reshape(width // 2, -1)
    back = (
        ring4(first_back, "y").reshape(width // 2, -1),
        ring4(second_back, "x").reshape(width // 2, -1),
    )
    weights = jnp.concatenate([first_in, second_in], 0)

    lanes = lax.broadcasted_iota(jnp.int32, (1, 128), 1)
    mine = (lanes == me) | (lanes == me + experts)
    share = jnp.sum(
        jnp.where(mine, arrived[:, width:].astype(F32), 0.0), axis=1, keepdims=True
    )
    group = arrived[:, :width]
    gate_pre = jnp.dot(group, weights[:, :hidden_width], preferred_element_type=F32)
    up_pre = jnp.dot(group, weights[:, hidden_width:], preferred_element_type=F32)
    hidden = (jax.nn.silu(gate_pre) * up_pre * share).astype(BF)

    by_core = hidden.reshape(z_count, cores, rows, hidden_width)
    by_core = jnp.concatenate([by_core, by_core], 0)
    start = (z + 9) % 16

    def of_core(which):
        turned = lax.dynamic_slice(
            by_core, (start, which, 0, 0), (z_count, 1, rows, hidden_width)
        )
        grouped = turned[:-1].reshape(len(FAR), 3, rows, hidden_width).swapaxes(0, 1)
        return jnp.concatenate(
            [grouped.reshape(-1, hidden_width), turned[-1, 0]]
        )

    home, away = of_core(core), of_core(1 - core)

    def paired(matrix):
        def tangent(part):
            return lax.dot_general(
                part, matrix, (((1,), (1,)), ((), ())), preferred_element_type=F32
            )

        other = swap_cores(tangent(away).astype(BF))
        return (tangent(home) + other.astype(F32)).astype(BF)

    def settle(pieces, flip):
        jv = to_absolute(sum(p.astype(F32) for p in pieces), y, x, flip)
        curved = (curvature[:, None, None, None] * jv).astype(BF).reshape(rows, -1)
        return jv.astype(BF), curved

    def spread_far(curved):
        return jnp.concatenate([fetch(curved, "z", o, 16) if o else curved for o in FAR])

    def outer(near, away_near):
        def product(left, right):
            return lax.dot_general(
                left, right, (((0,), (0,)), ((), ())), preferred_element_type=F32
            )

        return (product(near, home) + product(away_near, away)).astype(BF)

    near_0 = reduce_near(paired(back[0]), rows)
    parts_1 = after(paired(back[1]), *near_0)
    far_0 = reduce_far(*near_0)
    near_1 = reduce_near(parts_1, rows)
    out_0, curved_0 = settle(far_0, False)
    own_0 = spread_far(curved_0)
    near_1 = lax.optimization_barrier(near_1 + tuple(far_0))[: len(near_1)]
    far_1 = reduce_far(*near_1)
    near_0 = spread_near(own_0, rows)
    out_1, curved_1 = settle(far_1, True)
    own_1 = spread_far(after(curved_1, own_0))
    near_0 = jnp.concatenate(near_0)
    away_0 = swap_cores(near_0)
    near_1 = spread_near(after(own_1, near_0), rows)
    part_0 = outer(near_0, away_0)
    near_1 = jnp.concatenate(
        lax.optimization_barrier(near_1 + (part_0,))[: len(near_1)]
    )
    away_1 = swap_cores(near_1)
    product_0 = lax.psum_scatter(part_0, ("y", "x"), scatter_dimension=0, tiled=True)
    product_1 = outer(near_1, away_1)
    for axis in ("y", "x"):
        moved = lax.all_to_all(
            product_1.reshape(4, -1, hidden_width), axis, 0, 0, tiled=True
        )
        product_1 = jnp.sum(moved.astype(F32), axis=0).astype(BF)
    output_tangent = jnp.concatenate([out_0, out_1], 3).reshape(rows, width)
    return output_tangent, jnp.concatenate([product_0, product_1])[None]


def solution(mesh):
    torus = Mesh(mesh.devices.reshape(4, 4, 16, 2), ("y", "x", "z", "c"))
    tokens = P(("y", "x", "z", "c"), None)
    matrix = P(("z", "c"), ("y", "x"), None)
    return jax.shard_map(
        local,
        mesh=torus,
        in_specs=(tokens, tokens, tokens, P(("y", "x", "z", "c")), matrix, matrix, matrix),
        out_specs=(tokens, matrix),
        check_vma=False,
    )
```

```python
import jax
import jax.numpy as jnp
from jax import lax
from jax.sharding import Mesh, PartitionSpec as P

BF = jnp.bfloat16
F32 = jnp.float32


def fetch(value, axis, shift, size):
    return lax.ppermute(value, axis, [((i + shift) % size, i) for i in range(size)])


Z = ("zh", "zl")


def swap_cores(value):
    return lax.ppermute(value, "c", [(0, 1), (1, 0)])


def ring4(value, axis):
    half = value.shape[-2] // 2
    after = fetch(value, axis, 1, 4)
    before = fetch(value, axis, -1, 4)
    low = fetch(after[..., :half, :], axis, 1, 4)
    high = fetch(before[..., half:, :], axis, -1, 4)
    return jnp.stack([value, after, jnp.concatenate([low, high], -2), before])


def turn(value, axis, start):
    doubled = jnp.concatenate([value, value], axis)
    return lax.dynamic_slice_in_dim(doubled, start, value.shape[axis], axis)


def to_relative(value, y, x):
    rows, width = value.shape
    value = turn(turn(value.reshape(rows, 4, 4, width // 16), 1, y), 2, x)
    first, second = jnp.split(value, 2, axis=3)
    second = second.swapaxes(1, 2)
    return jnp.concatenate([first.reshape(rows, -1), second.reshape(rows, -1)], 1)


def reduce_near(parts):
    own, ahead, across, behind = jnp.split(parts, 4)
    half = across.shape[0] // 2
    low = fetch(across[:half], Z, -2, 16)
    high = fetch(across[half:], Z, 2, 16)
    ahead = fetch(ahead, Z, -1, 16)
    behind = fetch(behind, Z, 1, 16)
    across = jnp.concatenate([low, high])
    return sum(p.astype(F32) for p in (own, ahead, behind, across)).astype(BF)


def spread_near(own):
    half = own.shape[0] // 2
    low = fetch(own[:half], Z, 2, 16)
    high = fetch(own[half:], Z, -2, 16)
    ahead = fetch(own, Z, 1, 16)
    behind = fetch(own, Z, -1, 16)
    return jnp.concatenate([own, ahead, low, high, behind])


def to_absolute(value, y, x):
    rows, width = value.shape
    first, second = jnp.split(value, 2, axis=1)
    first = first.reshape(rows, 4, 4, width // 32)
    second = second.reshape(rows, 4, 4, width // 32).swapaxes(1, 2)
    both = jnp.concatenate([first, second], 3)
    return turn(turn(both, 1, (4 - y) % 4), 2, (4 - x) % 4).reshape(rows, width)


def local(tokens, routes, gates, curvature, w_gate, w_up, direction):
    rows, width = tokens.shape
    hidden_width = w_gate.shape[2]
    z_far, z_near, cores = (lax.axis_size(name) for name in ("zh", "zl", "c"))
    experts = z_far * z_near * cores
    y, x, core = lax.axis_index("y"), lax.axis_index("x"), lax.axis_index("c")
    me = lax.axis_index(("zh", "zl", "c"))

    chosen = routes[:, :, None] == jnp.arange(experts, dtype=jnp.int32)
    table = jnp.sum(jnp.where(chosen, gates[:, :, None], 0.0), axis=1)
    table_high = table.astype(BF)
    table_low = (table - table_high.astype(F32)).astype(BF)
    sent = jnp.concatenate(
        [
            to_relative(tokens, y, x),
            table_high,
            table_low,
            jnp.zeros((rows, 128 - 2 * experts), BF),
        ],
        1,
    )
    arrived = lax.all_gather(sent, ("zh", "zl", "c"), axis=0, tiled=True)

    stacked = jnp.concatenate([w_gate[0], w_up[0], direction[0]], 1)
    half = stacked.shape[0] // 2
    first = ring4(ring4(stacked[:half], "x"), "y")
    second = ring4(ring4(stacked[half:], "y"), "x")
    weights = jnp.concatenate(
        [first.reshape(width // 2, -1), second.reshape(width // 2, -1)], 0
    )

    lanes = lax.broadcasted_iota(jnp.int32, (1, 128), 1)
    mine = (lanes == me) | (lanes == me + experts)
    share = jnp.sum(
        jnp.where(mine, arrived[:, width:].astype(F32), 0.0), axis=1, keepdims=True
    )
    group = arrived[:, :width]
    gate_pre = jnp.dot(group, weights[:, :hidden_width], preferred_element_type=F32)
    up_pre = jnp.dot(
        group, weights[:, hidden_width : 2 * hidden_width], preferred_element_type=F32
    )
    hidden = (jax.nn.silu(gate_pre) * up_pre * share).astype(BF)

    near = lax.axis_index("zl")
    by_core = hidden.reshape(z_far, z_near, cores, rows, hidden_width)
    by_core = jnp.concatenate([by_core, by_core], 1)

    def of_core(which):
        turned = lax.dynamic_slice(
            by_core, (0, near, which, 0, 0), (z_far, z_near, 1, rows, hidden_width)
        )
        return turned[:, :, 0].swapaxes(0, 1).reshape(-1, hidden_width)

    home, away = of_core(core), of_core(1 - core)

    def tangent(part):
        return lax.dot_general(
            part,
            weights[:, 2 * hidden_width :],
            (((1,), (1,)), ((), ())),
            preferred_element_type=F32,
        )

    other = swap_cores(tangent(away).astype(BF))
    paired = (tangent(home) + other.astype(F32)).astype(BF)
    jv = lax.psum_scatter(reduce_near(paired), "zh", scatter_dimension=0, tiled=True)
    output_tangent = to_absolute(jv, y, x)
    curved = (curvature[:, None] * output_tangent.astype(F32)).astype(BF)
    spread = spread_near(lax.all_gather(curved, "zh", axis=0, tiled=True))
    spread_away = swap_cores(spread)

    def outer(left, right):
        return lax.dot_general(
            left, right, (((0,), (0,)), ((), ())), preferred_element_type=F32
        )

    part = (outer(spread, home) + outer(spread_away, away)).astype(BF)

    def add_over(value, axis):
        value = value.reshape(4, -1, hidden_width)
        moved = lax.all_to_all(value, axis, 0, 0, tiled=True)
        return jnp.sum(moved.astype(F32), axis=0).astype(BF)

    product = add_over(add_over(part, "y"), "x")
    return output_tangent, product[None]


def solution(mesh):
    torus = Mesh(mesh.devices.reshape(4, 4, 4, 4, 2), ("y", "x", "zh", "zl", "c"))
    tokens = P(("y", "x", "zh", "zl", "c"), None)
    matrix = P(("zh", "zl", "c"), ("y", "x"), None)
    return jax.shard_map(
        local,
        mesh=torus,
        in_specs=(tokens, tokens, tokens, P(("y", "x", "zh", "zl", "c")), matrix, matrix, matrix),
        out_specs=(tokens, matrix),
        check_vma=False,
    )
```

```python
import jax
import jax.numpy as jnp
from jax import lax
from jax.sharding import Mesh, PartitionSpec as P

BF = jnp.bfloat16
F32 = jnp.float32


def fetch(value, axis, shift, size):
    return lax.ppermute(value, axis, [((i + shift) % size, i) for i in range(size)])


def ring4(value, axis):
    half = value.shape[-2] // 2
    after = fetch(value, axis, 1, 4)
    before = fetch(value, axis, -1, 4)
    low = fetch(after[..., :half, :], axis, 1, 4)
    high = fetch(before[..., half:, :], axis, -1, 4)
    return jnp.stack([value, after, jnp.concatenate([low, high], -2), before])


def turn(value, axis, start):
    doubled = jnp.concatenate([value, value], axis)
    return lax.dynamic_slice_in_dim(doubled, start, value.shape[axis], axis)


def to_relative(value, y, x):
    rows, width = value.shape
    value = turn(turn(value.reshape(rows, 4, 4, width // 16), 1, y), 2, x)
    first, second = jnp.split(value, 2, axis=3)
    second = second.swapaxes(1, 2)
    return jnp.concatenate([first.reshape(rows, -1), second.reshape(rows, -1)], 1)


def to_absolute(value, y, x):
    rows, width = value.shape
    first, second = jnp.split(value, 2, axis=1)
    first = first.reshape(rows, 4, 4, width // 32)
    second = second.reshape(rows, 4, 4, width // 32).swapaxes(1, 2)
    both = jnp.concatenate([first, second], 3)
    return turn(turn(both, 1, (4 - y) % 4), 2, (4 - x) % 4).reshape(rows, width)


def local(tokens, routes, gates, curvature, w_gate, w_up, direction):
    rows, width = tokens.shape
    hidden_width = w_gate.shape[2]
    z_count, cores = lax.axis_size("z"), lax.axis_size("c")
    experts = z_count * cores
    y, x, core = lax.axis_index("y"), lax.axis_index("x"), lax.axis_index("c")
    me = lax.axis_index(("z", "c"))

    chosen = routes[:, :, None] == jnp.arange(experts, dtype=jnp.int32)
    table = jnp.sum(jnp.where(chosen, gates[:, :, None], 0.0), axis=1)
    table_high = table.astype(BF)
    table_low = (table - table_high.astype(F32)).astype(BF)
    sent = jnp.concatenate(
        [
            to_relative(tokens, y, x),
            table_high,
            table_low,
            jnp.zeros((rows, 128 - 2 * experts), BF),
        ],
        1,
    )
    arrived = lax.all_gather(sent, ("z", "c"), axis=0, tiled=True)

    stacked = jnp.concatenate([w_gate[0], w_up[0], direction[0]], 1)
    half = stacked.shape[0] // 2
    first = ring4(ring4(stacked[:half], "x"), "y")
    second = ring4(ring4(stacked[half:], "y"), "x")
    weights = jnp.concatenate(
        [first.reshape(width // 2, -1), second.reshape(width // 2, -1)], 0
    )

    lanes = lax.broadcasted_iota(jnp.int32, (1, 128), 1)
    mine = (lanes == me) | (lanes == me + experts)
    share = jnp.sum(
        jnp.where(mine, arrived[:, width:].astype(F32), 0.0), axis=1, keepdims=True
    )
    group = arrived[:, :width]
    gate_pre = jnp.dot(group, weights[:, :hidden_width], preferred_element_type=F32)
    up_pre = jnp.dot(
        group, weights[:, hidden_width : 2 * hidden_width], preferred_element_type=F32
    )
    hidden = (jax.nn.silu(gate_pre) * up_pre * share).astype(BF)

    by_core = hidden.reshape(z_count, cores, rows, hidden_width)
    away = lax.dynamic_index_in_dim(by_core, 1 - core, 1, False).reshape(-1, hidden_width)
    home = lax.dynamic_index_in_dim(by_core, core, 1, False).reshape(-1, hidden_width)

    def tangent(part):
        return lax.dot_general(
            part,
            weights[:, 2 * hidden_width :],
            (((1,), (1,)), ((), ())),
            preferred_element_type=F32,
        )

    other = lax.ppermute(tangent(away).astype(BF), "c", [(0, 1), (1, 0)])
    paired = (tangent(home) + other.astype(F32)).astype(BF)
    jv = lax.psum_scatter(paired, "z", scatter_dimension=0, tiled=True)
    output_tangent = to_absolute(jv, y, x)
    curved = curvature[:, None] * output_tangent.astype(F32)
    peak = jnp.max(jnp.abs(curved), axis=1, keepdims=True)
    power = jnp.floor(jnp.log2(jnp.maximum(peak, 1e-30)))
    scaled = jnp.concatenate(
        [curved * jnp.exp2(-power), jnp.broadcast_to(power, (rows, 128))], 1
    ).astype(jnp.float16)
    spread = lax.all_gather(scaled, ("z", "c"), axis=0, tiled=True)
    lifted = hidden.astype(F32) * jnp.exp2(spread[:, width : width + 1].astype(F32))
    part = lax.dot_general(
        spread[:, :width].astype(BF),
        lifted.astype(BF),
        (((0,), (0,)), ((), ())),
        preferred_element_type=F32,
    ).astype(BF)
    moved = lax.all_to_all(
        part.reshape(16, -1, hidden_width), ("y", "x"), 0, 0, tiled=True
    )
    product = jnp.sum(moved.astype(F32), axis=0).astype(BF)
    return output_tangent, product[None]


def solution(mesh):
    torus = Mesh(mesh.devices.reshape(4, 4, 16, 2), ("y", "x", "z", "c"))
    tokens = P(("y", "x", "z", "c"), None)
    matrix = P(("z", "c"), ("y", "x"), None)
    return jax.shard_map(
        local,
        mesh=torus,
        in_specs=(tokens, tokens, tokens, P(("y", "x", "z", "c")), matrix, matrix, matrix),
        out_specs=(tokens, matrix),
        check_vma=False,
    )
```

```python
import jax
import jax.numpy as jnp
from jax import lax
from jax.sharding import Mesh, PartitionSpec as P

BF = jnp.bfloat16
F32 = jnp.float32
HALF = jnp.float16


def to_half(value, lift):
    value = value.astype(F32)
    peak = jnp.max(jnp.abs(value), axis=1, keepdims=True)
    power = jnp.floor(jnp.log2(jnp.maximum(peak, 1e-30))) - lift
    return (value * jnp.exp2(-power)).astype(HALF), power


def local(tokens, routes, gates, curvature, w_gate, w_up, direction):
    rows, width = tokens.shape
    hidden_width = w_gate.shape[2]
    z_count, cores = lax.axis_size("z"), lax.axis_size("c")
    experts = z_count * cores
    core = lax.axis_index("c")
    me = lax.axis_index(("z", "c"))

    chosen = routes[:, :, None] == jnp.arange(experts, dtype=jnp.int32)
    table = jnp.sum(jnp.where(chosen, gates[:, :, None], 0.0), axis=1)
    table_high = table.astype(BF)
    table_low = (table - table_high.astype(F32)).astype(BF)
    sent = jnp.concatenate(
        [
            tokens,
            table_high,
            table_low,
            jnp.zeros((rows, 128 - 2 * experts), BF),
        ],
        1,
    )
    arrived = lax.all_gather(sent, ("z", "c"), axis=0, tiled=True)

    halves = [to_half(matrix[0], 13) for matrix in (w_gate, w_up, direction)]
    powers = jnp.concatenate([power for _, power in halves], 1)
    packed = jnp.concatenate(
        [half for half, _ in halves] + [jnp.pad(powers, ((0, 0), (0, 125))).astype(HALF)], 1
    )
    packed = lax.all_gather(packed, "x", axis=0, tiled=True)
    packed = lax.all_gather(packed, "y", axis=0, tiled=True)
    scales = jnp.exp2(packed[:, 3 * hidden_width :].astype(F32))

    def unpack(which):
        columns = packed[:, which * hidden_width : (which + 1) * hidden_width]
        return (columns.astype(F32) * scales[:, which : which + 1]).astype(BF)

    gate_matrix, up_matrix, back = lax.optimization_barrier(
        (unpack(0), unpack(1), unpack(2))
    )

    lanes = lax.broadcasted_iota(jnp.int32, (1, 128), 1)
    mine = (lanes == me) | (lanes == me + experts)
    share = jnp.sum(
        jnp.where(mine, arrived[:, width:].astype(F32), 0.0), axis=1, keepdims=True
    )
    group = arrived[:, :width]
    gate_pre = jnp.dot(group, gate_matrix, preferred_element_type=F32)
    up_pre = jnp.dot(group, up_matrix, preferred_element_type=F32)
    hidden = (jax.nn.silu(gate_pre) * up_pre * share).astype(BF)

    by_core = hidden.reshape(z_count, cores, rows, hidden_width)
    away = lax.dynamic_index_in_dim(by_core, 1 - core, 1, False).reshape(-1, hidden_width)
    home = lax.dynamic_index_in_dim(by_core, core, 1, False).reshape(-1, hidden_width)

    def tangent(part):
        return lax.dot_general(
            part, back, (((1,), (1,)), ((), ())), preferred_element_type=F32
        )

    other = lax.ppermute(tangent(away).astype(BF), "c", [(0, 1), (1, 0)])
    kept = lax.optimization_barrier(tangent(home))
    paired = (kept + other.astype(F32)).astype(BF)
    output_tangent = lax.psum_scatter(paired, "z", scatter_dimension=0, tiled=True)
    curved, power = to_half(curvature[:, None] * output_tangent.astype(F32), 13)
    scaled = jnp.concatenate(
        [curved, jnp.broadcast_to(power, (rows, 128)).astype(HALF)], 1
    )
    spread = lax.all_gather(scaled, ("z", "c"), axis=0, tiled=True)
    lifted = hidden.astype(F32) * jnp.exp2(spread[:, width : width + 1].astype(F32))
    part = lax.dot_general(
        spread[:, :width].astype(BF),
        lifted.astype(BF),
        (((0,), (0,)), ((), ())),
        preferred_element_type=F32,
    ).astype(BF)
    moved = lax.all_to_all(
        part.reshape(16, -1, hidden_width), ("y", "x"), 0, 0, tiled=True
    )
    product = jnp.sum(moved.astype(F32), axis=0).astype(BF)
    return output_tangent, product[None]


def solution(mesh):
    torus = Mesh(mesh.devices.reshape(4, 4, 16, 2), ("y", "x", "z", "c"))
    tokens = P(("y", "x", "z", "c"), None)
    matrix = P(("z", "c"), ("y", "x"), None)
    return jax.shard_map(
        local,
        mesh=torus,
        in_specs=(tokens, tokens, tokens, P(("y", "x", "z", "c")), matrix, matrix, matrix),
        out_specs=(tokens, matrix),
        check_vma=False,
    )
```

```python
import jax
import jax.numpy as jnp
from jax import lax
from jax.sharding import Mesh, PartitionSpec as P

BF = jnp.bfloat16
F32 = jnp.float32


def fetch(value, axis, shift, size):
    return lax.ppermute(value, axis, [((i + shift) % size, i) for i in range(size)])


def ring4(value, axis):
    half = value.shape[-2] // 2
    after = fetch(value, axis, 1, 4)
    before = fetch(value, axis, -1, 4)
    low = fetch(after[..., :half, :], axis, 1, 4)
    high = fetch(before[..., half:, :], axis, -1, 4)
    return [value, after, before], [low, high]


def ring4_stack(value, axis):
    soon, late = ring4(value, axis)
    return jnp.stack([soon[0], soon[1], jnp.concatenate(late, -2), soon[2]])


def turn(value, axis, start):
    doubled = jnp.concatenate([value, value], axis)
    return lax.dynamic_slice_in_dim(doubled, start, value.shape[axis], axis)


def to_relative(value, y, x):
    rows, width = value.shape
    value = turn(turn(value.reshape(rows, 4, 4, width // 16), 1, y), 2, x)
    first, second = jnp.split(value, 2, axis=3)
    pieces = []
    for part in (first, second.swapaxes(1, 2)):
        pieces += [part[:, :2], part[:, 3:]]
    pieces += [first[:, 2:3], second.swapaxes(1, 2)[:, 2:3]]
    return jnp.concatenate([piece.reshape(rows, -1) for piece in pieces], 1)


def to_absolute(value, y, x):
    rows, width = value.shape
    unit = width // 8
    a, b, c, d, e, f = jnp.split(
        value, [2 * unit, 3 * unit, 5 * unit, 6 * unit, 7 * unit], axis=1
    )
    first = jnp.concatenate([a, e, b], 1).reshape(rows, 4, 4, width // 32)
    second = jnp.concatenate([c, f, d], 1).reshape(rows, 4, 4, width // 32)
    both = jnp.concatenate([first, second.swapaxes(1, 2)], 3)
    return turn(turn(both, 1, (4 - y) % 4), 2, (4 - x) % 4).reshape(rows, width)


def local(tokens, routes, gates, curvature, w_gate, w_up, direction):
    rows, width = tokens.shape
    hidden_width = w_gate.shape[2]
    z_count, cores = lax.axis_size("z"), lax.axis_size("c")
    experts = z_count * cores
    y, x, core = lax.axis_index("y"), lax.axis_index("x"), lax.axis_index("c")
    me = lax.axis_index(("z", "c"))

    chosen = routes[:, :, None] == jnp.arange(experts, dtype=jnp.int32)
    table = jnp.sum(jnp.where(chosen, gates[:, :, None], 0.0), axis=1)
    table_high = table.astype(BF)
    table_low = (table - table_high.astype(F32)).astype(BF)
    sent = jnp.concatenate(
        [
            to_relative(tokens, y, x),
            table_high,
            table_low,
            jnp.zeros((rows, 128 - 2 * experts), BF),
        ],
        1,
    )
    arrived = lax.all_gather(sent, ("z", "c"), axis=0, tiled=True)

    stacked = jnp.concatenate([w_gate[0], w_up[0], direction[0]], 1)
    half = stacked.shape[0] // 2
    first_soon, first_late = ring4(ring4_stack(stacked[:half], "x"), "y")
    second_soon, second_late = ring4(ring4_stack(stacked[half:], "y"), "x")
    columns = stacked.shape[1]
    soon = jnp.concatenate([p.reshape(-1, columns) for p in first_soon + second_soon])

    lanes = lax.broadcasted_iota(jnp.int32, (1, 128), 1)
    mine = (lanes == me) | (lanes == me + experts)
    share = jnp.sum(
        jnp.where(mine, arrived[:, width:].astype(F32), 0.0), axis=1, keepdims=True
    )
    group = arrived[:, :width]
    early = soon.shape[0]

    def times(left, right, which):
        right = right[:, which * hidden_width : (which + 1) * hidden_width]
        return jnp.dot(left, right, preferred_element_type=F32)

    gate_soon = times(group[:, :early], soon, 0)
    up_soon = times(group[:, :early], soon, 1)
    low_1, high_1, low_2, high_2, gate_soon, up_soon = lax.optimization_barrier(
        (*first_late, *second_late, gate_soon, up_soon)
    )
    late = jnp.concatenate(
        [
            jnp.concatenate(pair, -2).reshape(-1, columns)
            for pair in ((low_1, high_1), (low_2, high_2))
        ]
    )
    back = jnp.concatenate([soon[:, 2 * hidden_width :], late[:, 2 * hidden_width :]])
    gate_pre = gate_soon + times(group[:, early:], late, 0)
    up_pre = up_soon + times(group[:, early:], late, 1)
    hidden = (jax.nn.silu(gate_pre) * up_pre * share).astype(BF)

    by_core = hidden.reshape(z_count, cores, rows, hidden_width)
    away = lax.dynamic_index_in_dim(by_core, 1 - core, 1, False).reshape(-1, hidden_width)
    home = lax.dynamic_index_in_dim(by_core, core, 1, False).reshape(-1, hidden_width)

    def tangent(part):
        return lax.dot_general(
            part, back, (((1,), (1,)), ((), ())), preferred_element_type=F32
        )

    other = lax.ppermute(tangent(away).astype(BF), "c", [(0, 1), (1, 0)])
    kept = lax.optimization_barrier(tangent(home))
    paired = (kept + other.astype(F32)).astype(BF)
    jv = lax.psum_scatter(paired, "z", scatter_dimension=0, tiled=True)
    output_tangent = to_absolute(jv, y, x)
    curved = curvature[:, None] * output_tangent.astype(F32)
    peak = jnp.max(jnp.abs(curved), axis=1, keepdims=True)
    power = jnp.floor(jnp.log2(jnp.maximum(peak, 1e-30)))
    scaled = jnp.concatenate(
        [curved * jnp.exp2(-power), jnp.broadcast_to(power, (rows, 128))], 1
    ).astype(jnp.float16)
    spread = lax.all_gather(scaled, ("z", "c"), axis=0, tiled=True)
    lifted = hidden.astype(F32) * jnp.exp2(spread[:, width : width + 1].astype(F32))
    part = lax.dot_general(
        spread[:, :width].astype(BF),
        lifted.astype(BF),
        (((0,), (0,)), ((), ())),
        preferred_element_type=F32,
    ).astype(BF)
    moved = lax.all_to_all(
        part.reshape(16, -1, hidden_width), ("y", "x"), 0, 0, tiled=True
    )
    product = jnp.sum(moved.astype(F32), axis=0).astype(BF)
    return output_tangent, product[None]


def solution(mesh):
    torus = Mesh(mesh.devices.reshape(4, 4, 16, 2), ("y", "x", "z", "c"))
    tokens = P(("y", "x", "z", "c"), None)
    matrix = P(("z", "c"), ("y", "x"), None)
    return jax.shard_map(
        local,
        mesh=torus,
        in_specs=(tokens, tokens, tokens, P(("y", "x", "z", "c")), matrix, matrix, matrix),
        out_specs=(tokens, matrix),
        check_vma=False,
    )
```

```python
import jax
import jax.numpy as jnp
from jax import lax
from jax.sharding import Mesh, PartitionSpec as P

BF = jnp.bfloat16
F32 = jnp.float32
Z = ("zh", "zl")


def fetch(value, axis, shift, size):
    return lax.ppermute(value, axis, [((i + shift) % size, i) for i in range(size)])


def ring4(value, axis):
    half = value.shape[-2] // 2
    after = fetch(value, axis, 1, 4)
    before = fetch(value, axis, -1, 4)
    low = fetch(after[..., :half, :], axis, 1, 4)
    high = fetch(before[..., half:, :], axis, -1, 4)
    return [value, after, before], [low, high]


def ring4_stack(value, axis):
    soon, late = ring4(value, axis)
    return jnp.stack([soon[0], soon[1], jnp.concatenate(late, -2), soon[2]])


def turn(value, axis, start):
    doubled = jnp.concatenate([value, value], axis)
    return lax.dynamic_slice_in_dim(doubled, start, value.shape[axis], axis)


def to_relative(value, y, x):
    rows, width = value.shape
    value = turn(turn(value.reshape(rows, 4, 4, width // 16), 1, y), 2, x)
    first, second = jnp.split(value, 2, axis=3)
    pieces = []
    for part in (first, second.swapaxes(1, 2)):
        pieces += [part[:, :2], part[:, 3:]]
    pieces += [first[:, 2:3], second.swapaxes(1, 2)[:, 2:3]]
    return jnp.concatenate([piece.reshape(rows, -1) for piece in pieces], 1)


def to_absolute(value, y, x):
    rows, width = value.shape
    unit = width // 8
    a, b, c, d, e, f = jnp.split(
        value, [2 * unit, 3 * unit, 5 * unit, 6 * unit, 7 * unit], axis=1
    )
    first = jnp.concatenate([a, e, b], 1).reshape(rows, 4, 4, width // 32)
    second = jnp.concatenate([c, f, d], 1).reshape(rows, 4, 4, width // 32)
    both = jnp.concatenate([first, second.swapaxes(1, 2)], 3)
    return turn(turn(both, 1, (4 - y) % 4), 2, (4 - x) % 4).reshape(rows, width)


def reduce_near(parts):
    own, ahead, across, behind = jnp.split(parts, 4)
    half = across.shape[0] // 2
    low = fetch(across[:half], Z, -2, 16)
    high = fetch(across[half:], Z, 2, 16)
    ahead = fetch(ahead, Z, -1, 16)
    behind = fetch(behind, Z, 1, 16)
    across = jnp.concatenate([low, high])
    return sum(p.astype(F32) for p in (own, ahead, behind, across)).astype(BF)


def reduce_far(total, rows):
    moved = lax.all_to_all(total.reshape(-1, rows, total.shape[1]), "zh", 0, 0, tiled=True)
    return jnp.sum(moved.astype(F32), axis=0)


def local(tokens, routes, gates, curvature, w_gate, w_up, direction):
    rows, width = tokens.shape
    hidden_width = w_gate.shape[2]
    z_far, z_near, cores = (lax.axis_size(name) for name in ("zh", "zl", "c"))
    z_count = z_far * z_near
    experts = z_count * cores
    y, x, core = lax.axis_index("y"), lax.axis_index("x"), lax.axis_index("c")
    me = lax.axis_index(("zh", "zl", "c"))

    chosen = routes[:, :, None] == jnp.arange(experts, dtype=jnp.int32)
    table = jnp.sum(jnp.where(chosen, gates[:, :, None], 0.0), axis=1)
    table_high = table.astype(BF)
    table_low = (table - table_high.astype(F32)).astype(BF)
    sent = jnp.concatenate(
        [
            to_relative(tokens, y, x),
            table_high,
            table_low,
            jnp.zeros((rows, 128 - 2 * experts), BF),
        ],
        1,
    )
    arrived = lax.all_gather(sent, ("zh", "zl", "c"), axis=0, tiled=True)

    stacked = jnp.concatenate([w_gate[0], w_up[0], direction[0]], 1)
    half = stacked.shape[0] // 2
    first_soon, first_late = ring4(ring4_stack(stacked[:half], "x"), "y")
    second_soon, second_late = ring4(ring4_stack(stacked[half:], "y"), "x")
    columns = stacked.shape[1]
    soon = jnp.concatenate([p.reshape(-1, columns) for p in first_soon + second_soon])

    lanes = lax.broadcasted_iota(jnp.int32, (1, 128), 1)
    mine = (lanes == me) | (lanes == me + experts)
    share = jnp.sum(
        jnp.where(mine, arrived[:, width:].astype(F32), 0.0), axis=1, keepdims=True
    )
    group = arrived[:, :width]
    early = soon.shape[0]

    def times(left, right, which):
        right = right[:, which * hidden_width : (which + 1) * hidden_width]
        return jnp.dot(left, right, preferred_element_type=F32)

    gate_soon = times(group[:, :early], soon, 0)
    up_soon = times(group[:, :early], soon, 1)
    low_1, high_1, low_2, high_2, gate_soon, up_soon = lax.optimization_barrier(
        (*first_late, *second_late, gate_soon, up_soon)
    )
    late = jnp.concatenate(
        [
            jnp.concatenate(pair, -2).reshape(-1, columns)
            for pair in ((low_1, high_1), (low_2, high_2))
        ]
    )
    back = jnp.concatenate([soon[:, 2 * hidden_width :], late[:, 2 * hidden_width :]])
    gate_pre = gate_soon + times(group[:, early:], late, 0)
    up_pre = up_soon + times(group[:, early:], late, 1)
    hidden = (jax.nn.silu(gate_pre) * up_pre * share).astype(BF)

    by_core = hidden.reshape(z_count, cores, rows, hidden_width)
    away = lax.dynamic_index_in_dim(by_core, 1 - core, 1, False).reshape(-1, hidden_width)
    home = lax.dynamic_index_in_dim(by_core, core, 1, False).reshape(-1, hidden_width)

    def tangent(part):
        return lax.dot_general(
            part, back, (((1,), (1,)), ((), ())), preferred_element_type=F32
        )

    other = lax.ppermute(tangent(away).astype(BF), "c", [(0, 1), (1, 0)])
    kept = lax.optimization_barrier(tangent(home))
    paired = (kept + other.astype(F32)).astype(BF)
    middle = width // 2
    one = lax.psum_scatter(paired[:, :middle], Z, scatter_dimension=0, tiled=True)
    turned = turn(
        paired[:, middle:].reshape(z_far, z_near, rows, width - middle),
        1,
        lax.axis_index("zl"),
    )
    turned = turned.swapaxes(0, 1).reshape(-1, width - middle)
    two = reduce_far(reduce_near(turned), rows).astype(BF)
    jv = jnp.concatenate([one, two], 1)
    output_tangent = to_absolute(jv, y, x)
    curved = curvature[:, None] * output_tangent.astype(F32)
    peak = jnp.max(jnp.abs(curved), axis=1, keepdims=True)
    power = jnp.floor(jnp.log2(jnp.maximum(peak, 1e-30)))
    scaled = jnp.concatenate(
        [curved * jnp.exp2(-power), jnp.broadcast_to(power, (rows, 128))], 1
    ).astype(jnp.float16)
    spread = lax.all_gather(scaled, ("zh", "zl", "c"), axis=0, tiled=True)
    lifted = hidden.astype(F32) * jnp.exp2(spread[:, width : width + 1].astype(F32))
    part = lax.dot_general(
        spread[:, :width].astype(BF),
        lifted.astype(BF),
        (((0,), (0,)), ((), ())),
        preferred_element_type=F32,
    ).astype(BF)
    moved = lax.all_to_all(
        part.reshape(16, -1, hidden_width), ("y", "x"), 0, 0, tiled=True
    )
    product = jnp.sum(moved.astype(F32), axis=0).astype(BF)
    return output_tangent, product[None]


def solution(mesh):
    torus = Mesh(mesh.devices.reshape(4, 4, 4, 4, 2), ("y", "x", "zh", "zl", "c"))
    tokens = P(("y", "x", "zh", "zl", "c"), None)
    matrix = P(("zh", "zl", "c"), ("y", "x"), None)
    return jax.shard_map(
        local,
        mesh=torus,
        in_specs=(tokens, tokens, tokens, P(("y", "x", "zh", "zl", "c")), matrix, matrix, matrix),
        out_specs=(tokens, matrix),
        check_vma=False,
    )
```

```python
import functools

import jax
import jax.numpy as jnp
from jax import lax
from jax.experimental import pallas as pl
from jax.experimental.pallas import tpu as pltpu
from jax.sharding import Mesh, PartitionSpec as P

BF = jnp.bfloat16
F32 = jnp.float32


def fetch(value, axis, shift, size):
    return lax.ppermute(value, axis, [((i + shift) % size, i) for i in range(size)])


def ring4(value, axis):
    half = value.shape[-2] // 2
    after = fetch(value, axis, 1, 4)
    before = fetch(value, axis, -1, 4)
    low = fetch(after[..., :half, :], axis, 1, 4)
    high = fetch(before[..., half:, :], axis, -1, 4)
    return [value, after, before], [low, high]


def ring4_stack(value, axis):
    soon, late = ring4(value, axis)
    return jnp.stack([soon[0], soon[1], jnp.concatenate(late, -2), soon[2]])


def turn(value, axis, start):
    doubled = jnp.concatenate([value, value], axis)
    return lax.dynamic_slice_in_dim(doubled, start, value.shape[axis], axis)


def to_relative(value, y, x):
    rows, width = value.shape
    value = turn(turn(value.reshape(rows, 4, 4, width // 16), 1, y), 2, x)
    first, second = jnp.split(value, 2, axis=3)
    pieces = []
    for part in (first, second.swapaxes(1, 2)):
        pieces += [part[:, :2], part[:, 3:]]
    pieces += [first[:, 2:3], second.swapaxes(1, 2)[:, 2:3]]
    return jnp.concatenate([piece.reshape(rows, -1) for piece in pieces], 1)


def to_absolute(value, y, x):
    rows, width = value.shape
    unit = width // 8
    a, b, c, d, e, f = jnp.split(
        value, [2 * unit, 3 * unit, 5 * unit, 6 * unit, 7 * unit], axis=1
    )
    first = jnp.concatenate([a, e, b], 1).reshape(rows, 4, 4, width // 32)
    second = jnp.concatenate([c, f, d], 1).reshape(rows, 4, 4, width // 32)
    both = jnp.concatenate([first, second.swapaxes(1, 2)], 3)
    return turn(turn(both, 1, (4 - y) % 4), 2, (4 - x) % 4).reshape(rows, width)


def expert_kernel(size, group_ref, mask_ref, *refs):
    pieces, hidden_ref, tangent_ref = refs[:-2], refs[-2], refs[-1]
    gate = jnp.zeros((group_ref.shape[0], size), F32)
    up = jnp.zeros((group_ref.shape[0], size), F32)
    start = 0
    for piece in pieces:
        depth = piece.shape[0]
        rows = group_ref[:, start : start + depth]
        gate += jnp.dot(rows, piece[:, :size], preferred_element_type=F32)
        up += jnp.dot(rows, piece[:, size : 2 * size], preferred_element_type=F32)
        start += depth
    share = jnp.sum(
        group_ref[:, start:].astype(F32) * mask_ref[...], axis=1, keepdims=True
    )
    hidden = (jax.nn.silu(gate) * up * share).astype(BF)
    hidden_ref[...] = hidden
    start = 0
    for piece in pieces:
        depth = piece.shape[0]
        tangent_ref[:, start : start + depth] = lax.dot_general(
            hidden,
            piece[:, 2 * size :],
            (((1,), (1,)), ((), ())),
            preferred_element_type=F32,
        ).astype(BF)
        start += depth


def local(tokens, routes, gates, curvature, w_gate, w_up, direction):
    rows, width = tokens.shape
    hidden_width = w_gate.shape[2]
    z_count, cores = lax.axis_size("z"), lax.axis_size("c")
    experts = z_count * cores
    y, x, core = lax.axis_index("y"), lax.axis_index("x"), lax.axis_index("c")
    me = lax.axis_index(("z", "c"))

    chosen = routes[:, :, None] == jnp.arange(experts, dtype=jnp.int32)
    table = jnp.sum(jnp.where(chosen, gates[:, :, None], 0.0), axis=1)
    table_high = table.astype(BF)
    table_low = (table - table_high.astype(F32)).astype(BF)
    sent = jnp.concatenate(
        [
            to_relative(tokens, y, x),
            table_high,
            table_low,
            jnp.zeros((rows, 128 - 2 * experts), BF),
        ],
        1,
    )
    arrived = lax.all_gather(sent, ("z", "c"), axis=0, tiled=True)

    stacked = jnp.concatenate([w_gate[0], w_up[0], direction[0]], 1)
    half = stacked.shape[0] // 2
    first_soon, first_late = ring4(ring4_stack(stacked[:half], "x"), "y")
    second_soon, second_late = ring4(ring4_stack(stacked[half:], "y"), "x")
    columns = stacked.shape[1]
    late = [
        jnp.concatenate(pair, -2).reshape(-1, columns) for pair in (first_late, second_late)
    ]
    pieces = [p.reshape(-1, columns) for p in first_soon + second_soon] + late

    lanes = lax.broadcasted_iota(jnp.int32, (1, 128), 1)
    mask = ((lanes == me) | (lanes == me + experts)).astype(F32)
    count, wide = arrived.shape
    block = count // 4
    hidden, tangents = pl.pallas_call(
        functools.partial(expert_kernel, hidden_width),
        grid=(4,),
        in_specs=[
            pl.BlockSpec((block, wide), lambda i: (i, 0)),
            pl.BlockSpec((1, 128), lambda i: (0, 0)),
        ]
        + [
            pl.BlockSpec(p.shape, lambda i: (0, 0), pipeline_mode=pl.Buffered(1))
            for p in pieces
        ],
        out_specs=[
            pl.BlockSpec((block, hidden_width), lambda i: (i, 0)),
            pl.BlockSpec((block, width), lambda i: (i, 0)),
        ],
        out_shape=[
            jax.ShapeDtypeStruct((count, hidden_width), BF),
            jax.ShapeDtypeStruct((count, width), BF),
        ],
        compiler_params=pltpu.CompilerParams(vmem_limit_bytes=52 * 1024 * 1024),
        cost_estimate=pl.CostEstimate(
            flops=6 * count * width * hidden_width,
            bytes_accessed=2 * (count * (2 * width + hidden_width) + 3 * width * hidden_width),
            transcendentals=count * hidden_width,
        ),
    )(arrived, mask, *pieces)

    by_core = tangents.reshape(z_count, cores, rows, width)
    away = lax.dynamic_index_in_dim(by_core, 1 - core, 1, False).reshape(-1, width)
    home = lax.dynamic_index_in_dim(by_core, core, 1, False).reshape(-1, width)
    other = lax.ppermute(away, "c", [(0, 1), (1, 0)])
    paired = (home.astype(F32) + other.astype(F32)).astype(BF)
    jv = lax.psum_scatter(paired, "z", scatter_dimension=0, tiled=True)
    output_tangent = to_absolute(jv, y, x)
    curved = curvature[:, None] * output_tangent.astype(F32)
    peak = jnp.max(jnp.abs(curved), axis=1, keepdims=True)
    power = jnp.floor(jnp.log2(jnp.maximum(peak, 1e-30)))
    scaled = jnp.concatenate(
        [curved * jnp.exp2(-power), jnp.broadcast_to(power, (rows, 128))], 1
    ).astype(jnp.float16)
    spread = lax.all_gather(scaled, ("z", "c"), axis=0, tiled=True)
    lifted = hidden.astype(F32) * jnp.exp2(spread[:, width : width + 1].astype(F32))
    part = lax.dot_general(
        spread[:, :width].astype(BF),
        lifted.astype(BF),
        (((0,), (0,)), ((), ())),
        preferred_element_type=F32,
    ).astype(BF)
    moved = lax.all_to_all(
        part.reshape(16, -1, hidden_width), ("y", "x"), 0, 0, tiled=True
    )
    product = jnp.sum(moved.astype(F32), axis=0).astype(BF)
    return output_tangent, product[None]


def solution(mesh):
    torus = Mesh(mesh.devices.reshape(4, 4, 16, 2), ("y", "x", "z", "c"))
    tokens = P(("y", "x", "z", "c"), None)
    matrix = P(("z", "c"), ("y", "x"), None)
    return jax.shard_map(
        local,
        mesh=torus,
        in_specs=(tokens, tokens, tokens, P(("y", "x", "z", "c")), matrix, matrix, matrix),
        out_specs=(tokens, matrix),
        check_vma=False,
    )
```

```python
import functools

import jax
import jax.numpy as jnp
from jax import lax
from jax.experimental import pallas as pl
from jax.experimental.pallas import tpu as pltpu
from jax.sharding import Mesh, PartitionSpec as P

BF = jnp.bfloat16
F32 = jnp.float32


def fetch(value, axis, shift, size):
    return lax.ppermute(value, axis, [((i + shift) % size, i) for i in range(size)])


def ring4(value, axis):
    half = value.shape[-2] // 2
    after = fetch(value, axis, 1, 4)
    before = fetch(value, axis, -1, 4)
    low = fetch(after[..., :half, :], axis, 1, 4)
    high = fetch(before[..., half:, :], axis, -1, 4)
    return [value, after, before], [low, high]


def ring4_stack(value, axis):
    soon, late = ring4(value, axis)
    return jnp.stack([soon[0], soon[1], jnp.concatenate(late, -2), soon[2]])


def turn(value, axis, start):
    doubled = jnp.concatenate([value, value], axis)
    return lax.dynamic_slice_in_dim(doubled, start, value.shape[axis], axis)


def to_relative(value, y, x):
    rows, width = value.shape
    value = turn(turn(value.reshape(rows, 4, 4, width // 16), 1, y), 2, x)
    first, second = jnp.split(value, 2, axis=3)
    pieces = []
    for part in (first, second.swapaxes(1, 2)):
        pieces += [part[:, :2], part[:, 3:]]
    pieces += [first[:, 2:3], second.swapaxes(1, 2)[:, 2:3]]
    return jnp.concatenate([piece.reshape(rows, -1) for piece in pieces], 1)


def to_absolute(value, y, x):
    rows, width = value.shape
    unit = width // 8
    a, b, c, d, e, f = jnp.split(
        value, [2 * unit, 3 * unit, 5 * unit, 6 * unit, 7 * unit], axis=1
    )
    first = jnp.concatenate([a, e, b], 1).reshape(rows, 4, 4, width // 32)
    second = jnp.concatenate([c, f, d], 1).reshape(rows, 4, 4, width // 32)
    both = jnp.concatenate([first, second.swapaxes(1, 2)], 3)
    return turn(turn(both, 1, (4 - y) % 4), 2, (4 - x) % 4).reshape(rows, width)


def expert_kernel(size, whole, group_ref, mask_ref, *refs):
    hidden_ref, tangent_ref = refs[-2], refs[-1]
    pieces = [(ref,) for ref in refs[:whole]]
    pieces += [refs[i : i + 2] for i in range(whole, len(refs) - 2, 2)]
    depth = pieces[0][0].shape[0]

    def matrix(piece, which):
        columns = slice(which * size, (which + 1) * size)
        if len(piece) == 1:
            return piece[0][:, columns]
        step = depth // 8
        return jnp.concatenate(
            [ref[i * step : (i + 1) * step, columns] for i in range(4) for ref in piece]
        )

    gate = jnp.zeros((group_ref.shape[0], size), F32)
    up = jnp.zeros((group_ref.shape[0], size), F32)
    for i, piece in enumerate(pieces):
        rows = group_ref[:, i * depth : (i + 1) * depth]
        gate += jnp.dot(rows, matrix(piece, 0), preferred_element_type=F32)
        up += jnp.dot(rows, matrix(piece, 1), preferred_element_type=F32)
    share = jnp.sum(
        group_ref[:, len(pieces) * depth :].astype(F32) * mask_ref[...],
        axis=1,
        keepdims=True,
    )
    hidden = (jax.nn.silu(gate) * up * share).astype(BF)
    hidden_ref[...] = hidden
    for i, piece in enumerate(pieces):
        tangent_ref[:, i * depth : (i + 1) * depth] = lax.dot_general(
            hidden,
            matrix(piece, 2),
            (((1,), (1,)), ((), ())),
            preferred_element_type=F32,
        ).astype(BF)


def local(tokens, routes, gates, curvature, w_gate, w_up, direction):
    rows, width = tokens.shape
    hidden_width = w_gate.shape[2]
    z_count, cores = lax.axis_size("z"), lax.axis_size("c")
    experts = z_count * cores
    y, x, core = lax.axis_index("y"), lax.axis_index("x"), lax.axis_index("c")
    me = lax.axis_index(("z", "c"))

    chosen = routes[:, :, None] == jnp.arange(experts, dtype=jnp.int32)
    table = jnp.sum(jnp.where(chosen, gates[:, :, None], 0.0), axis=1)
    table_high = table.astype(BF)
    table_low = (table - table_high.astype(F32)).astype(BF)
    sent = jnp.concatenate(
        [
            to_relative(tokens, y, x),
            table_high,
            table_low,
            jnp.zeros((rows, 128 - 2 * experts), BF),
        ],
        1,
    )
    arrived = lax.all_gather(sent, ("z", "c"), axis=0, tiled=True)

    stacked = jnp.concatenate([w_gate[0], w_up[0], direction[0]], 1)
    half = stacked.shape[0] // 2
    first_soon, first_late = ring4(ring4_stack(stacked[:half], "x"), "y")
    second_soon, second_late = ring4(ring4_stack(stacked[half:], "y"), "x")
    columns = stacked.shape[1]
    pieces = [
        p.reshape(-1, columns)
        for p in first_soon + second_soon + first_late + second_late
    ]
    whole = len(first_soon) + len(second_soon)

    lanes = lax.broadcasted_iota(jnp.int32, (1, 128), 1)
    mask = ((lanes == me) | (lanes == me + experts)).astype(F32)
    count, wide = arrived.shape
    block = count // 4
    hidden, tangents = pl.pallas_call(
        functools.partial(expert_kernel, hidden_width, whole),
        grid=(4,),
        in_specs=[
            pl.BlockSpec((block, wide), lambda i: (i, 0)),
            pl.BlockSpec((1, 128), lambda i: (0, 0)),
        ]
        + [
            pl.BlockSpec(p.shape, lambda i: (0, 0), pipeline_mode=pl.Buffered(1))
            for p in pieces
        ],
        out_specs=[
            pl.BlockSpec((block, hidden_width), lambda i: (i, 0)),
            pl.BlockSpec((block, width), lambda i: (i, 0)),
        ],
        out_shape=[
            jax.ShapeDtypeStruct((count, hidden_width), BF),
            jax.ShapeDtypeStruct((count, width), BF),
        ],
        compiler_params=pltpu.CompilerParams(vmem_limit_bytes=52 * 1024 * 1024),
        cost_estimate=pl.CostEstimate(
            flops=6 * count * width * hidden_width,
            bytes_accessed=2 * (count * (2 * width + hidden_width) + 3 * width * hidden_width),
            transcendentals=count * hidden_width,
        ),
    )(arrived, mask, *pieces)

    by_core = tangents.reshape(z_count, cores, rows, width)
    away = lax.dynamic_index_in_dim(by_core, 1 - core, 1, False).reshape(-1, width)
    home = lax.dynamic_index_in_dim(by_core, core, 1, False).reshape(-1, width)
    other = lax.ppermute(away, "c", [(0, 1), (1, 0)])
    paired = (home.astype(F32) + other.astype(F32)).astype(BF)
    jv = lax.psum_scatter(paired, "z", scatter_dimension=0, tiled=True)
    output_tangent = to_absolute(jv, y, x)
    curved = curvature[:, None] * output_tangent.astype(F32)
    peak = jnp.max(jnp.abs(curved), axis=1, keepdims=True)
    power = jnp.floor(jnp.log2(jnp.maximum(peak, 1e-30)))
    scaled = jnp.concatenate(
        [curved * jnp.exp2(-power), jnp.broadcast_to(power, (rows, 128))], 1
    ).astype(jnp.float16)
    spread = lax.all_gather(scaled, ("z", "c"), axis=0, tiled=True)
    lifted = hidden.astype(F32) * jnp.exp2(spread[:, width : width + 1].astype(F32))
    part = lax.dot_general(
        spread[:, :width].astype(BF),
        lifted.astype(BF),
        (((0,), (0,)), ((), ())),
        preferred_element_type=F32,
    ).astype(BF)
    moved = lax.all_to_all(
        part.reshape(16, -1, hidden_width), ("y", "x"), 0, 0, tiled=True
    )
    product = jnp.sum(moved.astype(F32), axis=0).astype(BF)
    return output_tangent, product[None]


def solution(mesh):
    torus = Mesh(mesh.devices.reshape(4, 4, 16, 2), ("y", "x", "z", "c"))
    tokens = P(("y", "x", "z", "c"), None)
    matrix = P(("z", "c"), ("y", "x"), None)
    return jax.shard_map(
        local,
        mesh=torus,
        in_specs=(tokens, tokens, tokens, P(("y", "x", "z", "c")), matrix, matrix, matrix),
        out_specs=(tokens, matrix),
        check_vma=False,
    )
```
